512 devices in a mesh: wide: 64 (over x, y, core), narrow: 8 (over z).
Axes of the slice: x: 4, y: 8, z: 8, core: 2. Of those that a mesh axis runs over, the one named last changes fastest.
Arguments:
- edge_msg: bfloat16 [131072, 1024], P(('wide', 'narrow')), may hold values from -6 to 6
- basis: bfloat16 [131072, 512], P(('wide', 'narrow')), may hold values from -1.5 to 1.5
- atom_h: bfloat16 [4096, 512], P('narrow'), may hold values from -6 to 6
- edge_source: int32 [131072], P(('wide', 'narrow')), may hold values from 0 to 4095
- edge_target: int32 [131072], P(('wide', 'narrow')), may hold values from 0 to 4095, as said below
- send_rows: int32 [512, 2048], P(('wide', 'narrow')), may hold values from 0 to 255
- trip_slot: int32 [131072, 32], P(('wide', 'narrow')), may hold values from 0 to 2047, as said below
- w_down: bfloat16 [1024, 64], replicated, may hold values from -0.1875 to 0.1875
- w_bil: bfloat16 [1024, 64], replicated, may hold values from -0.1875 to 0.1875
- w_up: bfloat16 [64, 1024], replicated, may hold values from -0.75 to 0.75
- w_atom_in: bfloat16 [1024, 512], replicated, may hold values from -0.1875 to 0.1875
- atom_gain: float32 [512], replicated, may hold values from 0.5 to 1.5
- w_atom: bfloat16 [512, 512], replicated, may hold values from -0.25 to 0.25
- w_src: bfloat16 [512, 1024], replicated, may hold values from -0.25 to 0.25
- w_tgt: bfloat16 [512, 1024], replicated, may hold values from -0.25 to 0.25
Outputs:
- edge_out: bfloat16 [131072, 1024], P(('wide', 'narrow'))
- atom_out: bfloat16 [4096, 512], P('narrow')
The draws below stay inside these ranges and needn't reach their ends.
Inputs may be any that keep to these rules, and one draw needn't show every extreme that they name: `edge_target`: the edges of block b target atoms of the narrow block b % 8, that is (b % 8) * 512 to (b % 8 + 1) * 512 - 1, never outside that range, and never falling (sorted) within a block. `trip_slot`: for each receiving block and each wide index p, the slots p * 32 + c that its triplets use form a prefix c < count of 1 to 32 entries; every block has some p with all 32 used.
All inputs are finite; a program needn't handle non-finite values.
Results may differ from the reference program's by a relative error of at most 0.0065.
Values may be sent and summed in bfloat16 or wider, within the bound.
A program may use at most 64 MiB of HBM per device.

```python
import jax
import jax.numpy as jnp
from jax import lax

DE = 1024
DT = 64
NB = 16
DA = 512
TRIP = 32
CAP = 32
EDEV = 256
ADEV = 512
EDGES = 131072
ATOMS = 4096
N_WIDE = 64
N_NARROW = 8
DEVICES = 512


def draw_edge_target(key, part):
    blocks = N_WIDE * N_NARROW
    lowest = jnp.arange(blocks, dtype=jnp.int32) % N_NARROW * ADEV
    picks = jax.random.randint(jax.random.fold_in(key, 11), (blocks, EDEV), 0, ADEV, dtype=jnp.int32)
    picks = jnp.sort(picks, axis=1) + lowest[:, None]
    return picks.reshape(-1).astype(jnp.int32)


def draw_trip_slot(key, part):
    blocks = N_WIDE * N_NARROW
    counts = jax.random.randint(jax.random.fold_in(key, 21), (blocks, N_WIDE), 1, CAP + 1, dtype=jnp.int32)
    hottest = jax.random.randint(jax.random.fold_in(key, 22), (blocks, 1), 0, N_WIDE, dtype=jnp.int32)
    counts = jnp.where(jnp.arange(N_WIDE, dtype=jnp.int32)[None, :] == hottest, CAP, counts)
    totals = jnp.cumsum(counts, axis=1).astype(jnp.int32)
    picks = jax.random.randint(jax.random.fold_in(key, 23), (blocks, EDEV * TRIP), 0, totals[:, -1:], dtype=jnp.int32)
    owner = jax.vmap(lambda edges, values: jnp.searchsorted(edges, values, side='right'))(totals, picks).astype(jnp.int32)
    starts = jnp.take_along_axis(totals - counts, owner, axis=1)
    slots = owner * CAP + (picks - starts)
    return slots.reshape(EDGES, TRIP).astype(jnp.int32)


def plant(array, key, low, top_value):
    shape = array.shape
    place = [jax.random.randint(jax.random.fold_in(key, axis), (), 0, shape[axis]) for axis in range(len(shape))]
    array = array.at[tuple(place)].set(low)
    longest = shape.index(max(shape))
    place[longest] = (place[longest] + 1) % shape[longest]
    return array.at[tuple(place)].set(top_value)


def block_scale(key, shape, shards, smallest, largest):
    loudness, own = 1.0, jax.random.fold_in(key, 6)
    for position, parts in shards:
        heights = jnp.exp(jax.random.uniform(jax.random.fold_in(own, position), (parts,), jnp.float32, smallest / len(shards), largest / len(shards)))
        loudness = loudness * jnp.repeat(heights, shape[position] // parts).reshape([-1 if axis == position else 1 for axis in range(len(shape))])
    return loudness


def bell_draw(key, shape, spread, bound, split=(), held_as=jnp.bfloat16):
    values = jax.random.normal(key, shape, jnp.float32) * spread
    if len(split) > 0:
        values = block_scale(key, shape, split, -0.22, 0.18) * values
    return jnp.clip(values, min=-bound, max=bound).astype(held_as)


def setup_inputs(seed: int = 0) -> dict:
    seeds = jax.random.split(jax.random.key(seed), 16)
    return {
        "edge_msg": bell_draw(seeds[0], (EDGES, DE), 1.0, 6.0, ((0, 512),)),
        "basis": bell_draw(seeds[1], (EDGES, TRIP * NB), 0.25, 1.5, ((0, 512),)),
        "atom_h": bell_draw(seeds[2], (ATOMS, DA), 1.0, 6.0, ((0, 8),)),
        "edge_source": plant(jax.random.randint(seeds[3], (EDGES,), 0, ATOMS), jax.random.fold_in(seeds[3], 1), 0, ATOMS - 1).astype(jnp.int32),
        "edge_target": draw_edge_target(jax.random.fold_in(seeds[15], 71), 0),
        "send_rows": plant(jax.random.randint(seeds[5], (DEVICES, N_WIDE * CAP), 0, EDEV), jax.random.fold_in(seeds[5], 1), 0, EDEV - 1).astype(jnp.int32),
        "trip_slot": draw_trip_slot(jax.random.fold_in(seeds[15], 71), 0),
        "w_down": bell_draw(seeds[7], (DE, DT), DE ** -0.5, 0.1875),
        "w_bil": bell_draw(seeds[8], (NB * DT, DT), (NB * DT) ** -0.5, 0.1875),
        "w_up": bell_draw(seeds[9], (DT, DE), DT ** -0.5, 0.75),
        "w_atom_in": bell_draw(seeds[10], (DE, DA), DE ** -0.5, 0.1875),
        "atom_gain": jnp.clip(1.0 + 0.1 * jax.random.normal(seeds[11], (DA,), jnp.float32), 0.5, 1.5),
        "w_atom": bell_draw(seeds[12], (DA, DA), DA ** -0.5, 0.25),
        "w_src": bell_draw(seeds[13], (DA, DE), DA ** -0.5, 0.25),
        "w_tgt": bell_draw(seeds[14], (DA, DE), DA ** -0.5, 0.25),
    }


def silu(value):
    return value / (1.0 + jnp.exp(-value))

def reference(edge_msg, basis, atom_h, edge_source, edge_target, send_rows, trip_slot, w_down, w_bil, w_up, w_atom_in, atom_gain, w_atom, w_src, w_tgt):
    blocks = N_WIDE * N_NARROW
    down = silu(jnp.dot(edge_msg, w_down, preferred_element_type=jnp.float32)).astype(jnp.bfloat16)

    def mix_block(inputs):
        slots, values, block = inputs
        receiver_wide = block // N_NARROW
        narrow_index = block % N_NARROW
        sender = slots // CAP * N_NARROW + narrow_index
        local_edge = send_rows[sender, receiver_wide * CAP + slots % CAP]
        edge_ids = (sender * EDEV + local_edge).astype(jnp.int32)
        other = down[edge_ids].astype(jnp.float32)
        weights = values.reshape(EDEV, TRIP, NB).astype(jnp.float32)
        mixed = jnp.einsum('etk,etc->ekc', weights, other)
        return mixed.reshape(EDEV, NB * DT).astype(jnp.bfloat16)
    mixed = lax.map(mix_block, (trip_slot.reshape(blocks, EDEV, TRIP), basis.reshape(blocks, EDEV, TRIP * NB), jnp.arange(blocks, dtype=jnp.int32)))
    mixed = mixed.reshape(EDGES, NB * DT)
    trip = silu(jnp.dot(mixed, w_bil, preferred_element_type=jnp.float32)).astype(jnp.bfloat16)
    edge_mid = (edge_msg.astype(jnp.float32) + jnp.dot(trip, w_up, preferred_element_type=jnp.float32)).astype(jnp.bfloat16)
    message = jnp.dot(edge_mid, w_atom_in, preferred_element_type=jnp.float32).astype(jnp.bfloat16)
    atom_sum = jax.ops.segment_sum(message.astype(jnp.float32), edge_target, num_segments=ATOMS)
    scale = lax.rsqrt(lax.optimization_barrier(jnp.mean(atom_sum * atom_sum, axis=-1, keepdims=True)) + 1e-06)
    normed = (atom_sum * scale * atom_gain).astype(jnp.bfloat16)
    atom_out = (atom_h.astype(jnp.float32) + silu(jnp.dot(normed, w_atom, preferred_element_type=jnp.float32))).astype(jnp.bfloat16)
    source_rows = atom_out[edge_source]
    target_rows = atom_out[edge_target]
    update = jnp.dot(source_rows, w_src, preferred_element_type=jnp.float32) + jnp.dot(target_rows, w_tgt, preferred_element_type=jnp.float32)
    edge_out = (edge_mid.astype(jnp.float32) + silu(update)).astype(jnp.bfloat16)
    return (edge_out, atom_out)
```

```python
import jax
import jax.numpy as jnp
from jax import lax
from jax.experimental import pallas as pl
from jax.experimental.pallas import tpu as pltpu
from jax.sharding import PartitionSpec as P

MESH = pl.DeviceIdType.MESH
BF16, F32, I32 = jnp.bfloat16, jnp.float32, jnp.int32
NX, NY, NZ = 4, 8, 8
WIDE = NX * NY * 2
EDGES, WIDTH, TRIP, BASIS, TRIPLETS, SLOTS = 256, 1024, 64, 16, 32, 32
ATOMS, ATOM_WIDTH, HALF, TILE = 512, 512, 256, 128


def silu(value):
    return value / (1.0 + jnp.exp(-value))


def dot(a, b):
    return jnp.dot(a, b, preferred_element_type=F32)


def iota(shape, dim):
    return lax.broadcasted_iota(I32, shape, dim)


def ones_where(mask):
    return jnp.where(mask, 1.0, 0.0).astype(BF16)


def remote(src, dst, send_sem, recv_sem, device):
    return pltpu.make_async_remote_copy(
        src_ref=src, dst_ref=dst, send_sem=send_sem, recv_sem=recv_sem,
        device_id=device, device_id_type=MESH,
    )


def mix_kernel(
    msg_ref, basis_ref, slot_ref, rows_ref, target_ref, w_down_ref, w_bil_ref, w_up_ref, w_in_ref,
    mid_ref, part_ref,
    out_buf, in_buf, table, spread, bands, q_buf, g_buf, mixed, send_sem, recv_sem,
):
    me, row = lax.axis_index("wide"), lax.axis_index("narrow")
    barrier = pltpu.get_barrier_semaphore()

    def greet(i, carry):
        pl.semaphore_signal(barrier, inc=1, device_id=(lax.rem(me + i, WIDE), row), device_id_type=MESH)
        return carry

    lax.fori_loop(1, WIDE, greet, 0)

    down = silu(dot(msg_ref[...], w_down_ref[...])).T
    twice = jnp.concatenate([down, down], axis=0).astype(BF16)
    low_lane = iota((16, TILE), 1) < TRIP
    for j in range(8):
        hot = ones_where(iota((EDGES, 256), 0) == rows_ref[:, j * 256 : (j + 1) * 256])
        picked = dot(twice, hot).T
        for p in range(8):
            first, second = picked[p * 32 : p * 32 + 16], picked[p * 32 + 16 : p * 32 + 32]
            out_buf[j * 8 + p] = jnp.where(low_lane, first, second).astype(BF16)

    pl.semaphore_wait(barrier, WIDE - 1)

    def copy_to(i):
        peer = lax.rem(me + i, WIDE)
        return peer, remote(out_buf.at[peer], in_buf.at[me], send_sem.at[peer], recv_sem.at[me], (peer, row))

    def send(i, carry):
        copy_to(i)[1].start()
        return carry

    lax.fori_loop(1, WIDE, send, 0)
    in_buf[me] = out_buf[me]

    spread[...] = ones_where((iota((512, 256), 0) >> 4) == (iota((512, 256), 1) & 31))
    key = iota((8, 512), 1) & 15
    band = (iota((TILE, 256), 0) & 7) == (iota((TILE, 256), 1) >> 5)

    def build(i, carry):
        two = basis_ref[pl.ds(pl.multiple_of(i * 16, 16), 16), :].astype(F32)
        for h in range(2):
            x = two[h * 8 : h * 8 + 8]
            tall = jnp.concatenate([jnp.where(key == k, x, 0.0) for k in range(BASIS)], axis=0)
            block = jnp.where(band, dot(tall.astype(BF16), spread[...]), 0.0)
            bands[pl.ds(pl.multiple_of(i * 256 + h * TILE, TILE), TILE), :] = block.astype(BF16)
        return carry

    lax.fori_loop(0, EDGES // 16, build, 0)

    slots = slot_ref[...]
    spread2 = ones_where(iota((TRIPLETS, 256), 0) == (iota((TRIPLETS, 256), 1) & 31))
    band2 = (iota((EDGES, 256), 0) & 7) == (iota((EDGES, 256), 1) >> 5)

    def flat(values):
        wide = jnp.where(band2, dot(values.astype(F32).astype(BF16), spread2), 0.0)
        return wide.reshape(EDGES // 8, 8, 256).sum(axis=1)

    q_buf[...] = (flat((slots >> 5) & 31) * 16.0 + flat(slots & 15)).astype(I32)
    g_buf[...] = flat(((slots >> 10) << 1) | ((slots >> 4) & 1)).astype(I32)

    def arrived(i, carry):
        peer = lax.rem(me + i, WIDE)
        remote(out_buf.at[peer], in_buf.at[peer], send_sem.at[peer], recv_sem.at[peer], (peer, row)).wait_recv()
        return carry

    lax.fori_loop(1, WIDE, arrived, 0)

    received = in_buf[...].reshape(WIDE * 16, TILE).astype(F32)
    table[...] = jnp.concatenate([received[:512].T, received[512:].T], axis=0).astype(BF16)
    low_lane8 = iota((8, TILE), 1) < TRIP

    def mix(i, carry):
        q, g = q_buf[pl.ds(i, 1), :], g_buf[pl.ds(i, 1), :]
        hot = ones_where(iota((512, 256), 0) == q)
        four = dot(table[...], hot)
        other = jnp.where(
            g < 2,
            jnp.where(g == 0, four[0:64], four[64:128]),
            jnp.where(g == 2, four[128:192], four[192:256]),
        )
        other = jnp.concatenate([other, other], axis=0).astype(BF16)
        block = bands[pl.ds(pl.multiple_of(i * TILE, TILE), TILE), :]
        got = lax.dot_general(block, other, (((1,), (1,)), ((), ())), preferred_element_type=F32)
        for k in range(8):
            pair = jnp.where(low_lane8, got[k * 16 : k * 16 + 8], got[k * 16 + 8 : k * 16 + 16])
            mixed[pl.ds(pl.multiple_of(i * 8, 8), 8), k * TILE : (k + 1) * TILE] = pair
        return carry

    lax.fori_loop(0, EDGES // 8, mix, 0)

    trip = silu(dot(mixed[...].astype(BF16), w_bil_ref[...])).astype(BF16)
    mid = (msg_ref[...].astype(F32) + dot(trip, w_up_ref[...])).astype(BF16)
    mid_ref[...] = mid
    message = dot(mid, w_in_ref[...]).astype(BF16)
    hot = ones_where(iota((ATOMS, EDGES), 0) == target_ref[...] - row * ATOMS)
    part_ref[...] = dot(hot, message)

    def sent(i, carry):
        copy_to(i)[1].wait_send()
        return carry

    lax.fori_loop(1, WIDE, sent, 0)


def atom_kernel(
    part_ref, mid_ref, source_ref, target_ref, atom_ref, gain_ref, w_atom_ref, w_src_ref, w_tgt_ref,
    edge_out, atom_out,
    snd1, rcv1, snd2, rcv2, snd3, rcv3, snd4, rcv4, all_a, all_b, sib_a, sib_b, src_sib, pick_snd, pick_rcv, col,
    s1, r1, s2, r2, s3, r3, s4, r4, si, ri, sa1, ra1, sb1, rb1, sa2, ra2, sb2, rb2, sring, rring, so, ro, sp, rp,
):
    wide, z = lax.axis_index("wide"), lax.axis_index("narrow")
    x, y, c = wide // 16, (wide // 2) % NY, wide % 2
    other = 1 - c

    def at(px, py, pc, pz):
        return (px * 16 + py * 2 + pc, pz)

    sibling = at(x, y, other, z)
    xs = [(lax.rem(x + i, NX), i) for i in range(1, NX)]
    ys = [(lax.rem(y + i, NY), i) for i in range(1, NY)]
    zs = [(lax.rem(z + i, NZ), i) for i in range(1, NZ)]
    peers = (
        [sibling]
        + [at(p, y, c, z) for p, _ in xs]
        + [at(x, p, c, z) for p, _ in ys]
        + [at(x, y, c, p) for p, _ in zs]
    )
    barrier = pltpu.get_barrier_semaphore()
    for peer in peers:
        pl.semaphore_signal(barrier, inc=1, device_id=peer, device_id_type=MESH)

    mine, theirs = pl.ds(pl.multiple_of(c * HALF, HALF), HALF), pl.ds(pl.multiple_of(other * HALF, HALF), HALF)
    snd1[...] = part_ref[:, theirs].astype(BF16)
    pl.semaphore_wait(barrier, len(peers))

    waiting = []

    def start(copy):
        copy.start()
        waiting.append(copy)

    start(remote(snd1, rcv1, s1, r1, sibling))
    start(remote(source_ref, src_sib, si, ri, sibling))
    remote(snd1, rcv1, s1, r1, sibling).wait_recv()

    sums = part_ref[:, mine] + rcv1[...].astype(F32)
    snd2[...] = sums.astype(BF16).reshape(NX, NY * 16, HALF)
    for p, _ in xs:
        start(remote(snd2.at[p], rcv2.at[x], s2.at[p], r2.at[x], at(p, y, c, z)))
    my_x = pl.ds(pl.multiple_of(x * TILE, TILE), TILE)
    total = part_ref[my_x, mine] + rcv1[my_x, :].astype(F32)
    for p, _ in xs:
        remote(snd2.at[p], rcv2.at[p], s2.at[p], r2.at[p], at(p, y, c, z)).wait_recv()
        total = total + rcv2[p].astype(F32)
    snd3[...] = total.astype(BF16).reshape(NY, 16, HALF)
    for p, _ in ys:
        start(remote(snd3.at[p], rcv3.at[y], s3.at[p], r3.at[y], at(x, p, c, z)))
    share = snd3[y].astype(F32)
    for p, _ in ys:
        remote(snd3.at[p], rcv3.at[p], s3.at[p], r3.at[p], at(x, p, c, z)).wait_recv()
        share = share + rcv3[p].astype(F32)
    snd4[...] = share
    start(remote(snd4, rcv4, s4, r4, sibling))

    remote(source_ref, src_sib, si, ri, sibling).wait_recv()
    for i, ref in enumerate((source_ref, src_sib, target_ref)):
        for h in range(2):
            line = ref[:, h * TILE : (h + 1) * TILE].astype(F32)
            turned = jnp.broadcast_to(line, (TILE, TILE)).T
            col[i * 2 + h] = turned.astype(I32)

    remote(snd4, rcv4, s4, r4, sibling).wait_recv()
    theirs4 = rcv4[...]
    squares = jnp.sum(share * share, axis=-1, keepdims=True) + jnp.sum(theirs4 * theirs4, axis=-1, keepdims=True)
    scale = lax.rsqrt(squares * (1.0 / ATOM_WIDTH) + 1e-06)
    norm_mine = (share * scale * gain_ref[:, mine]).astype(BF16)
    norm_theirs = (theirs4 * scale * gain_ref[:, theirs]).astype(BF16)
    grown = silu(dot(norm_mine, w_atom_ref[mine, mine]) + dot(norm_theirs, w_atom_ref[theirs, mine]))
    first = pl.multiple_of(x * TILE + y * 16, 16)
    fresh = (atom_ref[pl.ds(first, 16), mine].astype(F32) + grown).astype(BF16)
    all_a[z, x, y] = fresh[:, :TILE]
    all_b[z, x, y] = fresh[:, TILE:]

    for p, _ in xs:
        start(remote(all_a.at[z, x, y], all_a.at[z, x, y], sa1.at[p], ra1.at[x], at(p, y, c, z)))
    for p, _ in zs:
        start(remote(all_b.at[z, x, y], all_b.at[z, x, y], sb1.at[p], rb1.at[z], at(x, y, c, p)))
    for p, _ in xs:
        block = all_a.at[z, p, y]
        remote(block, block, sa1.at[p], ra1.at[p], at(p, y, c, z)).wait_recv()
    for p, _ in ys:
        block = all_a.at[z, :, y]
        start(remote(block, block, sa2.at[p], ra2.at[y], at(x, p, c, z)))
    for p, _ in zs:
        block = all_b.at[p, x, y]
        remote(block, block, sb1.at[p], rb1.at[p], at(x, y, c, p)).wait_recv()
    for p, _ in xs:
        block = all_b.at[:, x, y]
        start(remote(block, block, sb2.at[p], rb2.at[x], at(p, y, c, z)))

    def ring_copy(axis, way, step, half, sending):
        n, pos = (NZ, z) if axis == 0 else (NY, y)
        hop = 1 if way == 0 else n - 1
        back = step - 1 if sending else step
        block = lax.rem(pos + (n - back if way == 0 else back), n)
        part = pl.ds(half * 2, 2)
        view = all_a.at[block, part] if axis == 0 else all_b.at[:, part, block]
        to = lax.rem(pos + hop, n)
        device = at(x, y, c, to) if axis == 0 else at(x, to, c, z)
        index = ((axis * 2 + way) * 4 + step - 1) * 2 + half
        return remote(view, view, sring.at[index], rring.at[index], device)

    for p, _ in xs:
        block = all_b.at[:, p, y]
        remote(block, block, sb2.at[p], rb2.at[p], at(p, y, c, z)).wait_recv()
    for half in range(2):
        for way in range(2):
            start(ring_copy(1, way, 1, half, True))
    for p, _ in ys:
        block = all_a.at[z, :, p]
        remote(block, block, sa2.at[p], ra2.at[p], at(x, p, c, z)).wait_recv()
    for half in range(2):
        for way in range(2):
            start(ring_copy(0, way, 1, half, True))
    own_a = remote(all_a.at[z], sib_a, so.at[0], ro.at[0], sibling)
    start(own_a)
    for step in range(1, 5):
        for half in range(2):
            for axis in (1, 0):
                for way in range(2):
                    if step == 4 and half != way:
                        continue
                    ring_copy(axis, way, step, half, False).wait_recv()
                    if step < 3 or (step == 3 and half == way):
                        start(ring_copy(axis, way, step + 1, half, True))
    own_b = remote(all_b.at[z], sib_b, so.at[1], ro.at[1], sibling)
    start(own_b)

    lanes = iota((EDGES, ATOMS), 1)

    def column(i):
        halves = [jnp.concatenate([col[i * 2 + h]] * (ATOMS // TILE), axis=1) for h in range(2)]
        return jnp.concatenate(halves, axis=0)

    def rows_of(first_ref, second_ref):
        a, b = first_ref[...].reshape(ATOMS, TILE), second_ref[...].reshape(ATOMS, TILE)
        return jnp.concatenate([a, b], axis=1)

    def picked(i):
        total = jnp.zeros((EDGES, HALF), F32)
        for block in range(NZ):
            hot = ones_where(column(i) - block * ATOMS == lanes)
            total = total + dot(hot, rows_of(all_a.at[block], all_b.at[block]))
        return total.astype(BF16)

    pick_snd[...] = picked(1)
    start(remote(pick_snd, pick_rcv, sp, rp, sibling))
    update = dot(picked(0), w_src_ref[mine, :])
    own_a.wait_recv()
    own_b.wait_recv()
    hot = ones_where(column(2) - z * ATOMS == lanes)
    ours = rows_of(all_a.at[z], all_b.at[z])
    sibs = rows_of(sib_a, sib_b)
    atom_out[:, mine] = ours
    atom_out[:, theirs] = sibs
    update += dot(dot(hot, ours).astype(BF16), w_tgt_ref[mine, :])
    update += dot(dot(hot, sibs).astype(BF16), w_tgt_ref[theirs, :])
    remote(pick_snd, pick_rcv, sp, rp, sibling).wait_recv()
    update += dot(pick_rcv[...], w_src_ref[theirs, :])
    edge_out[...] = (mid_ref[...].astype(F32) + silu(update)).astype(BF16)
    for copy in waiting:
        copy.wait_send()


def dma(*shape):
    return pltpu.SemaphoreType.DMA(shape)


def per_device(
    edge_msg, basis, atom_h, edge_source, edge_target, send_rows, trip_slot,
    w_down, w_bil, w_up, w_atom_in, atom_gain, w_atom, w_src, w_tgt,
):
    vmem = pl.BlockSpec(memory_space=pltpu.VMEM)
    source = edge_source.reshape(1, EDGES)
    target = edge_target.reshape(1, EDGES)
    mid, partial = pl.pallas_call(
        mix_kernel,
        out_shape=(
            jax.ShapeDtypeStruct((EDGES, WIDTH), BF16),
            jax.ShapeDtypeStruct((ATOMS, ATOM_WIDTH), F32),
        ),
        in_specs=[vmem] * 9,
        out_specs=(vmem, vmem),
        scratch_shapes=[
            pltpu.VMEM((WIDE, 16, TILE), BF16),
            pltpu.VMEM((WIDE, 16, TILE), BF16),
            pltpu.VMEM((256, 512), BF16),
            pltpu.VMEM((512, 256), BF16),
            pltpu.VMEM((EDGES * BASIS, 256), BF16),
            pltpu.VMEM((EDGES // 8, 256), I32),
            pltpu.VMEM((EDGES // 8, 256), I32),
            pltpu.VMEM((EDGES, BASIS * TRIP), F32),
            dma(WIDE),
            dma(WIDE),
        ],
        compiler_params=pltpu.CompilerParams(
            collective_id=0, has_side_effects=True, vmem_limit_bytes=40 * 1024 * 1024
        ),
        name="mix",
    )(edge_msg, basis, trip_slot, send_rows, target, w_down, w_bil, w_up, w_atom_in)

    def every():
        return pltpu.VMEM((NZ, NX, NY, 16, TILE), BF16)

    def one():
        return pltpu.VMEM((NX, NY, 16, TILE), BF16)

    edge_out, atom_out = pl.pallas_call(
        atom_kernel,
        out_shape=(
            jax.ShapeDtypeStruct((EDGES, WIDTH), BF16),
            jax.ShapeDtypeStruct((ATOMS, ATOM_WIDTH), BF16),
        ),
        in_specs=[vmem] * 9,
        out_specs=(vmem, vmem),
        scratch_shapes=[
            pltpu.VMEM((ATOMS, HALF), BF16), pltpu.VMEM((ATOMS, HALF), BF16),
            pltpu.VMEM((NX, NY * 16, HALF), BF16), pltpu.VMEM((NX, NY * 16, HALF), BF16),
            pltpu.VMEM((NY, 16, HALF), BF16), pltpu.VMEM((NY, 16, HALF), BF16),
            pltpu.VMEM((16, HALF), F32), pltpu.VMEM((16, HALF), F32),
            every(), every(), one(), one(),
            pltpu.VMEM((1, EDGES), I32),
            pltpu.VMEM((EDGES, HALF), BF16), pltpu.VMEM((EDGES, HALF), BF16),
            pltpu.VMEM((6, TILE, TILE), I32),
            pltpu.SemaphoreType.DMA, pltpu.SemaphoreType.DMA,
            dma(NX), dma(NX), dma(NY), dma(NY),
            pltpu.SemaphoreType.DMA, pltpu.SemaphoreType.DMA,
            pltpu.SemaphoreType.DMA, pltpu.SemaphoreType.DMA,
            dma(NX), dma(NX), dma(NZ), dma(NZ), dma(NY), dma(NY), dma(NX), dma(NX),
            dma(32), dma(32), dma(2), dma(2),
            pltpu.SemaphoreType.DMA, pltpu.SemaphoreType.DMA,
        ],
        compiler_params=pltpu.CompilerParams(
            collective_id=1, has_side_effects=True, vmem_limit_bytes=40 * 1024 * 1024
        ),
        name="atoms",
    )(partial, mid, source, target, atom_h, atom_gain.reshape(1, ATOM_WIDTH), w_atom, w_src, w_tgt)
    return edge_out, atom_out


def solution(mesh):
    placed = (
        P(("wide", "narrow"), None),
        P(("wide", "narrow"), None),
        P("narrow", None),
        P(("wide", "narrow")),
        P(("wide", "narrow")),
        P(("wide", "narrow"), None),
        P(("wide", "narrow"), None),
        P(), P(), P(), P(), P(), P(), P(), P(),
    )
    return jax.shard_map(
        per_device,
        mesh=mesh,
        in_specs=placed,
        out_specs=(P(("wide", "narrow"), None), P("narrow", None)),
        check_vma=False,
    )
```

```python
import jax
import jax.numpy as jnp
from jax import lax
from jax.experimental import pallas as pl
from jax.experimental.pallas import tpu as pltpu
from jax.sharding import PartitionSpec as P

MESH = pl.DeviceIdType.MESH
BF16, F32, I32 = jnp.bfloat16, jnp.float32, jnp.int32
NX, NY, NZ = 4, 8, 8
WIDE = NX * NY * 2
EDGES, WIDTH, TRIP, BASIS, TRIPLETS, SLOTS = 256, 1024, 64, 16, 32, 32
ATOMS, ATOM_WIDTH, HALF, TILE = 512, 512, 256, 128
GROUP = 32


def silu(value):
    return value / (1.0 + jnp.exp(-value))


def dot(a, b):
    return jnp.dot(a, b, preferred_element_type=F32)


def iota(shape, dim):
    return lax.broadcasted_iota(I32, shape, dim)


def dot_t(a, b):
    return lax.dot_general(a, b, (((1,), (1,)), ((), ())), preferred_element_type=F32)


def ones_where(mask):
    return jnp.where(mask, 1.0, 0.0).astype(BF16)


def remote(src, dst, send_sem, recv_sem, device):
    return pltpu.make_async_remote_copy(
        src_ref=src, dst_ref=dst, send_sem=send_sem, recv_sem=recv_sem,
        device_id=device, device_id_type=MESH,
    )


def kernel(
    source_ref, target_ref, gain_ref, msg_hbm, rows_hbm, w_down_hbm, basis_hbm, slot_hbm, w_bil_hbm, w_up_hbm,
    w_in_hbm, w_src_hbm, w_tgt_hbm, w_atom_hbm, atom_hbm,
    edge_out, atom_out,
    msg_ref, rows_ref, w_down_ref, basis_ref, slot_ref, w_bil_ref, w_up_ref, w_in_ref, w_src_ref, w_tgt_ref,
    w_atom_ref, atom_ref, load_sem,
    out_buf, in_buf, table, spread, bands, digit_buf, where_buf, mixed, send_sem, recv_sem, mid_ref, part_ref,
    snd1, rcv1, snd2, rcv2, snd3, rcv3, snd4, rcv4, all_a, all_b, sib_a, sib_b, src_sib, pick_snd, pick_rcv, col,
    s1, r1, s2, r2, s3, r3, s4, r4, si, ri, sa1, ra1, sb1, rb1, sa2, ra2, sb2, rb2, sring, rring, so, ro, sp, rp,
):
    me, row = lax.axis_index("wide"), lax.axis_index("narrow")
    x, y, c, z = me // 16, (me // 2) % NY, me % 2, row
    other = 1 - c
    barrier = pltpu.get_barrier_semaphore()

    def at(px, py, pc, pz):
        return (px * 16 + py * 2 + pc, pz)

    sibling = at(x, y, other, z)
    xs = [(lax.rem(x + i, NX), i) for i in range(1, NX)]
    ys = [(lax.rem(y + i, NY), i) for i in range(1, NY)]
    zs = [(lax.rem(z + i, NZ), i) for i in range(1, NZ)]
    waiting = []

    def start(copy):
        copy.start()
        waiting.append(copy)

    def greet(i, carry):
        pl.semaphore_signal(barrier, inc=1, device_id=(lax.rem(me + i, WIDE), row), device_id_type=MESH)
        return carry

    lax.fori_loop(1, WIDE, greet, 0)
    for p, _ in zs:
        pl.semaphore_signal(barrier, inc=1, device_id=at(x, y, c, p), device_id_type=MESH)

    mine, theirs = pl.ds(pl.multiple_of(c * HALF, HALF), HALF), pl.ds(pl.multiple_of(other * HALF, HALF), HALF)
    my_rows = pl.ds(pl.multiple_of(x * TILE + y * 16, 16), 16)
    pairs = [
        (msg_hbm, msg_ref), (w_down_hbm, w_down_ref), (rows_hbm, rows_ref), (basis_hbm, basis_ref),
        (slot_hbm, slot_ref), (w_bil_hbm, w_bil_ref), (w_up_hbm, w_up_ref), (w_in_hbm, w_in_ref),
        (w_atom_hbm.at[:, mine], w_atom_ref), (atom_hbm.at[my_rows, mine], atom_ref),
        (w_src_hbm, w_src_ref), (w_tgt_hbm, w_tgt_ref),
    ]
    loads = [pltpu.make_async_copy(a, b, load_sem.at[i]) for i, (a, b) in enumerate(pairs)]
    for load in loads:
        load.start()
    for load in loads[:3]:
        load.wait()

    down = silu(dot_t(w_down_ref[...], msg_ref[...]))
    twice = jnp.concatenate([down, down], axis=0).astype(BF16)
    low_lane = iota((16, TILE), 1) < TRIP
    for j in range(8):
        hot = ones_where(iota((EDGES, 256), 0) == rows_ref[:, j * 256 : (j + 1) * 256])
        picked = dot(twice, hot).T
        for p in range(8):
            first, second = picked[p * 32 : p * 32 + 16], picked[p * 32 + 16 : p * 32 + 32]
            out_buf[j * 8 + p] = jnp.where(low_lane, first, second).astype(BF16)

    pl.semaphore_wait(barrier, WIDE - 1 + NZ - 1)
    start(remote(source_ref, src_sib, si, ri, sibling))
    def copy_to(i):
        peer = lax.rem(me + i, WIDE)
        return peer, remote(out_buf.at[peer], in_buf.at[me], send_sem.at[peer], recv_sem.at[me], (peer, row))

    def send(i, carry):
        copy_to(i)[1].start()
        return carry

    lax.fori_loop(1, WIDE, send, 0)
    in_buf[me] = out_buf[me]

    for load in loads[3:5]:
        load.wait()
    spread[...] = ones_where((iota((512, 256), 0) >> 4) == (iota((512, 256), 1) & 31))
    key = iota((8, 512), 1) & 15
    band = (iota((TILE, 256), 0) & 7) == (iota((TILE, 256), 1) >> 5)

    def build(i, carry):
        two = basis_ref[pl.ds(pl.multiple_of(i * 16, 16), 16), :].astype(F32)
        for h in range(2):
            x = two[h * 8 : h * 8 + 8]
            tall = jnp.concatenate([jnp.where(key == k, x, 0.0) for k in range(BASIS)], axis=0)
            block = jnp.where(band, dot(tall.astype(BF16), spread[...]), 0.0)
            bands[pl.ds(pl.multiple_of(i * 256 + h * TILE, TILE), TILE), :] = block.astype(BF16)
        return carry

    lax.fori_loop(0, EDGES // 16, build, 0, unroll=2)

    slots = slot_ref[...]
    parts = [(slots >> 5) & 31, slots & 15, ((slots >> 10) << 1) | ((slots >> 4) & 1), slots * 0]
    digits = jnp.concatenate(parts, axis=0).astype(F32).T
    digit = iota((TILE, 256), 0) >> 5
    left = iota((TILE, 256), 1) < TILE
    weigh = jnp.where(left & (digit == 0), 16.0, jnp.where(digit == jnp.where(left, 1, 2), 1.0, 0.0)).astype(BF16)
    own_digit = (iota((TRIPLETS, TILE), 1) & 31) == iota((TRIPLETS, TILE), 0)
    digit_buf[...] = digits

    def place(i, carry):
        few = digit_buf[pl.ds(pl.multiple_of(i * 8, 8), 8), :]
        tall = [jnp.where(own_digit, few[e : e + 1], 0.0) for e in range(8)]
        where_buf[pl.ds(pl.multiple_of(i * 256, 256), 256), :] = dot(
            jnp.concatenate(tall, axis=0).astype(BF16), weigh
        )
        return carry

    lax.fori_loop(0, EDGES // 8, place, 0, unroll=2)

    remote(source_ref, src_sib, si, ri, sibling).wait_recv()
    for i, ref in enumerate((source_ref, src_sib, target_ref)):
        for h in range(2):
            line = ref[:, h * TILE : (h + 1) * TILE].astype(F32)
            turned = jnp.broadcast_to(line, (TILE, TILE)).T
            col[i * 2 + h] = turned.astype(I32)

    def arrived(i, carry):
        peer = lax.rem(me + i, WIDE)
        remote(out_buf.at[peer], in_buf.at[peer], send_sem.at[peer], recv_sem.at[peer], (peer, row)).wait_recv()
        return carry

    lax.fori_loop(1, WIDE, arrived, 0)

    received = in_buf[...].reshape(WIDE * 16, TILE)
    table[...] = jnp.concatenate([received[:512], received[512:]], axis=1)
    low_lane8 = iota((8, TILE), 1) < TRIP
    lane = iota((GROUP * TRIPLETS, TILE), 1).astype(F32)
    lane_half = (iota((GROUP * TRIPLETS, TILE), 1) >> 6).astype(F32)

    def mix(i, carry):
        lines = pl.ds(pl.multiple_of(i * GROUP * TRIPLETS, GROUP * TRIPLETS), GROUP * TRIPLETS)
        q, g = where_buf[lines, :TILE], where_buf[lines, TILE:]
        hot = jnp.concatenate([ones_where(q == lane + float(j * TILE)) for j in range(4)], axis=1)
        four = dot(hot, table[...])
        rows = jnp.where(g == lane_half, four[:, :TILE], 0.0) + jnp.where(g == lane_half + 2.0, four[:, TILE:], 0.0)
        rows = rows.astype(BF16)
        for b in range(GROUP // 8):
            block = bands[pl.ds(pl.multiple_of((i * (GROUP // 8) + b) * TILE, TILE), TILE), :]
            got = dot(block, rows[b * 256 : (b + 1) * 256])
            got = got + pltpu.roll(got, TRIP, 1)
            for k in range(8):
                pair = jnp.where(low_lane8, got[k * 16 : k * 16 + 8], got[k * 16 + 8 : k * 16 + 16])
                mixed[pl.ds(pl.multiple_of(i * GROUP + b * 8, 8), 8), k * TILE : (k + 1) * TILE] = pair
        return carry

    lax.fori_loop(0, EDGES // GROUP, mix, 0)

    for load in loads[5:]:
        load.wait()
    trip = silu(dot_t(mixed[...].astype(BF16), w_bil_ref[...])).astype(BF16)
    mid = (msg_ref[...].astype(F32) + dot(trip, w_up_ref[...])).astype(BF16)
    mid_ref[...] = mid
    message = dot(mid, w_in_ref[...]).astype(BF16)
    hot = ones_where(iota((ATOMS, EDGES), 0) == target_ref[...] - row * ATOMS)
    part_ref[...] = dot(hot, message)

    my_x = pl.ds(pl.multiple_of(x * TILE, TILE), TILE)
    order = [p for p, _ in xs] + [x]

    def chip_copy(i, p):
        return remote(snd1.at[i], rcv1.at[i], s1.at[i], r1.at[i], sibling)

    for i, p in enumerate(order):
        snd1[i] = part_ref[pl.ds(pl.multiple_of(p * TILE, TILE), TILE), theirs].astype(BF16)
        start(chip_copy(i, p))
    for i, p in enumerate(order):
        chip_copy(i, p).wait_recv()
        if i < NX - 1:
            rows = part_ref[pl.ds(pl.multiple_of(p * TILE, TILE), TILE), mine] + rcv1[i].astype(F32)
            snd2[i] = rows.astype(BF16)
            start(remote(snd2.at[i], rcv2.at[x], s2.at[i], r2.at[x], at(p, y, c, z)))
    total = part_ref[my_x, mine] + rcv1[NX - 1].astype(F32)
    for p, _ in xs:
        remote(snd2.at[0], rcv2.at[p], s2.at[0], r2.at[p], at(p, y, c, z)).wait_recv()
        total = total + rcv2[p].astype(F32)
    snd3[...] = total.astype(BF16).reshape(NY, 16, HALF)
    for p, _ in ys:
        start(remote(snd3.at[p], rcv3.at[y], s3.at[p], r3.at[y], at(x, p, c, z)))
    share = snd3[y].astype(F32)
    for p, _ in ys:
        remote(snd3.at[p], rcv3.at[p], s3.at[p], r3.at[p], at(x, p, c, z)).wait_recv()
        share = share + rcv3[p].astype(F32)
    snd4[...] = share
    start(remote(snd4, rcv4, s4, r4, sibling))


    remote(snd4, rcv4, s4, r4, sibling).wait_recv()
    theirs4 = rcv4[...]
    squares = jnp.sum(share * share, axis=-1, keepdims=True) + jnp.sum(theirs4 * theirs4, axis=-1, keepdims=True)
    scale = lax.rsqrt(squares * (1.0 / ATOM_WIDTH) + 1e-06)
    norm_mine = (share * scale * gain_ref[:, mine]).astype(BF16)
    norm_theirs = (theirs4 * scale * gain_ref[:, theirs]).astype(BF16)
    grown = silu(dot(norm_mine, w_atom_ref[mine, :]) + dot(norm_theirs, w_atom_ref[theirs, :]))
    fresh = (atom_ref[...].astype(F32) + grown).astype(BF16)
    all_a[z, x, y] = fresh[:, :TILE]
    all_b[z, x, y] = fresh[:, TILE:]

    for p, _ in xs:
        start(remote(all_a.at[z, x, y], all_a.at[z, x, y], sa1.at[p], ra1.at[x], at(p, y, c, z)))
    for p, _ in zs:
        start(remote(all_b.at[z, x, y], all_b.at[z, x, y], sb1.at[p], rb1.at[z], at(x, y, c, p)))
    for p, _ in xs:
        block = all_a.at[z, p, y]
        remote(block, block, sa1.at[p], ra1.at[p], at(p, y, c, z)).wait_recv()
    for p, _ in ys:
        block = all_a.at[z, :, y]
        start(remote(block, block, sa2.at[p], ra2.at[y], at(x, p, c, z)))
    for p, _ in zs:
        block = all_b.at[p, x, y]
        remote(block, block, sb1.at[p], rb1.at[p], at(x, y, c, p)).wait_recv()
    for p, _ in xs:
        block = all_b.at[:, x, y]
        start(remote(block, block, sb2.at[p], rb2.at[x], at(p, y, c, z)))

    def ring_copy(axis, way, step, part, sending):
        n, pos = (NZ, z) if axis == 0 else (NY, y)
        hop = 1 if way == 0 else n - 1
        back = step - 1 if sending else step
        block = lax.rem(pos + (n - back if way == 0 else back), n)
        view = all_a.at[block, part] if axis == 0 else all_b.at[:, part, block]
        to = lax.rem(pos + hop, n)
        device = at(x, y, c, to) if axis == 0 else at(x, to, c, z)
        index = ((axis * 2 + way) * 4 + step - 1) * NX + part
        return remote(view, view, sring.at[index], rring.at[index], device)

    for p, _ in xs:
        block = all_b.at[:, p, y]
        remote(block, block, sb2.at[p], rb2.at[p], at(p, y, c, z)).wait_recv()
    for part in range(NX):
        for way in range(2):
            start(ring_copy(1, way, 1, part, True))
    for p, _ in ys:
        block = all_a.at[z, :, p]
        remote(block, block, sa2.at[p], ra2.at[p], at(x, p, c, z)).wait_recv()
    for part in range(NX):
        for way in range(2):
            start(ring_copy(0, way, 1, part, True))
    own_a = remote(all_a.at[z], sib_a, so.at[0], ro.at[0], sibling)
    start(own_a)
    for step in range(1, 5):
        for part in range(NX):
            for axis in (1, 0):
                for way in range(2):
                    last = part // 2 == way
                    if step == 4 and not last:
                        continue
                    ring_copy(axis, way, step, part, False).wait_recv()
                    if step < 3 or (step == 3 and last):
                        start(ring_copy(axis, way, step + 1, part, True))
    own_b = remote(all_b.at[z], sib_b, so.at[1], ro.at[1], sibling)
    start(own_b)

    lanes = iota((EDGES, ATOMS), 1)

    def column(i):
        halves = [jnp.concatenate([col[i * 2 + h]] * (ATOMS // TILE), axis=1) for h in range(2)]
        return jnp.concatenate(halves, axis=0)

    def rows_of(first_ref, second_ref):
        a, b = first_ref[...].reshape(ATOMS, TILE), second_ref[...].reshape(ATOMS, TILE)
        return jnp.concatenate([a, b], axis=1)

    def picked(i):
        total = jnp.zeros((EDGES, HALF), F32)
        for block in range(NZ):
            hot = ones_where(column(i) - block * ATOMS == lanes)
            total = total + dot(hot, rows_of(all_a.at[block], all_b.at[block]))
        return total.astype(BF16)

    pick_snd[...] = picked(1)
    start(remote(pick_snd, pick_rcv, sp, rp, sibling))
    update = dot(picked(0), w_src_ref[mine, :])
    own_a.wait_recv()
    own_b.wait_recv()
    hot = ones_where(column(2) - z * ATOMS == lanes)
    ours = rows_of(all_a.at[z], all_b.at[z])
    sibs = rows_of(sib_a, sib_b)
    atom_out[:, mine] = ours
    atom_out[:, theirs] = sibs
    update += dot(dot(hot, ours).astype(BF16), w_tgt_ref[mine, :])
    update += dot(dot(hot, sibs).astype(BF16), w_tgt_ref[theirs, :])
    remote(pick_snd, pick_rcv, sp, rp, sibling).wait_recv()
    update += dot(pick_rcv[...], w_src_ref[theirs, :])
    edge_out[...] = (mid_ref[...].astype(F32) + silu(update)).astype(BF16)
    for copy in waiting:
        copy.wait_send()

    def sent(i, carry):
        copy_to(i)[1].wait_send()
        return carry

    lax.fori_loop(1, WIDE, sent, 0)


def dma(*shape):
    return pltpu.SemaphoreType.DMA(shape)


def per_device(
    edge_msg, basis, atom_h, edge_source, edge_target, send_rows, trip_slot,
    w_down, w_bil, w_up, w_atom_in, atom_gain, w_atom, w_src, w_tgt,
):
    vmem = pl.BlockSpec(memory_space=pltpu.VMEM)
    hbm = pl.BlockSpec(memory_space=pltpu.HBM)

    def every():
        return pltpu.VMEM((NZ, NX, NY, 16, TILE), BF16)

    def one():
        return pltpu.VMEM((NX, NY, 16, TILE), BF16)

    def semaphores(n):
        return [pltpu.SemaphoreType.DMA] * n

    edge_out, atom_out = pl.pallas_call(
        kernel,
        out_shape=(
            jax.ShapeDtypeStruct((EDGES, WIDTH), BF16),
            jax.ShapeDtypeStruct((ATOMS, ATOM_WIDTH), BF16),
        ),
        in_specs=[vmem] * 3 + [hbm] * 12,
        out_specs=(vmem, vmem),
        scratch_shapes=[
            pltpu.VMEM((EDGES, WIDTH), BF16),
            pltpu.VMEM((1, WIDE * SLOTS), I32),
            pltpu.VMEM((TRIP, WIDTH), BF16),
            pltpu.VMEM((EDGES, TRIPLETS * BASIS), BF16),
            pltpu.VMEM((TRIPLETS, EDGES), I32),
            pltpu.VMEM((TRIP, BASIS * TRIP), BF16),
            pltpu.VMEM((TRIP, WIDTH), BF16),
            pltpu.VMEM((WIDTH, ATOM_WIDTH), BF16),
            pltpu.VMEM((ATOM_WIDTH, WIDTH), BF16),
            pltpu.VMEM((ATOM_WIDTH, WIDTH), BF16),
            pltpu.VMEM((ATOM_WIDTH, HALF), BF16),
            pltpu.VMEM((16, HALF), BF16),
            dma(12),
            pltpu.VMEM((WIDE, 16, TILE), BF16),
            pltpu.VMEM((WIDE, 16, TILE), BF16),
            pltpu.VMEM((512, 256), BF16),
            pltpu.VMEM((512, 256), BF16),
            pltpu.VMEM((EDGES * BASIS, 256), BF16),
            pltpu.VMEM((EDGES, TILE), F32),
            pltpu.VMEM((EDGES * TRIPLETS, 256), F32),
            pltpu.VMEM((EDGES, BASIS * TRIP), F32),
            dma(WIDE),
            dma(WIDE),
            pltpu.VMEM((EDGES, WIDTH), BF16),
            pltpu.VMEM((ATOMS, ATOM_WIDTH), F32),
            pltpu.VMEM((NX, TILE, HALF), BF16), pltpu.VMEM((NX, TILE, HALF), BF16),
            pltpu.VMEM((NX, NY * 16, HALF), BF16), pltpu.VMEM((NX, NY * 16, HALF), BF16),
            pltpu.VMEM((NY, 16, HALF), BF16), pltpu.VMEM((NY, 16, HALF), BF16),
            pltpu.VMEM((16, HALF), F32), pltpu.VMEM((16, HALF), F32),
            every(), every(), one(), one(),
            pltpu.VMEM((1, EDGES), I32),
            pltpu.VMEM((EDGES, HALF), BF16), pltpu.VMEM((EDGES, HALF), BF16),
            pltpu.VMEM((6, TILE, TILE), I32),
            dma(NX), dma(NX), dma(NX), dma(NX), dma(NY), dma(NY),
            *semaphores(4),
            dma(NX), dma(NX), dma(NZ), dma(NZ), dma(NY), dma(NY), dma(NX), dma(NX),
            dma(64), dma(64), dma(2), dma(2),
            *semaphores(2),
        ],
        compiler_params=pltpu.CompilerParams(
            collective_id=0, has_side_effects=True, vmem_limit_bytes=60 * 1024 * 1024
        ),
        name="block",
    )(
        edge_source.reshape(1, EDGES), edge_target.reshape(1, EDGES), atom_gain.reshape(1, ATOM_WIDTH),
        edge_msg, send_rows, w_down.T, basis, trip_slot.T, w_bil.T, w_up, w_atom_in, w_src, w_tgt, w_atom, atom_h,
    )
    return edge_out, atom_out


def solution(mesh):
    placed = (
        P(("wide", "narrow"), None),
        P(("wide", "narrow"), None),
        P("narrow", None),
        P(("wide", "narrow")),
        P(("wide", "narrow")),
        P(("wide", "narrow"), None),
        P(("wide", "narrow"), None),
        P(), P(), P(), P(), P(), P(), P(), P(),
    )
    return jax.shard_map(
        per_device,
        mesh=mesh,
        in_specs=placed,
        out_specs=(P(("wide", "narrow"), None), P("narrow", None)),
        check_vma=False,
    )
```

```python
import jax
import jax.numpy as jnp
from jax import lax
from jax.experimental import pallas as pl
from jax.experimental.pallas import tpu as pltpu
from jax.sharding import PartitionSpec as P

MESH = pl.DeviceIdType.MESH
BF16, F32, I32 = jnp.bfloat16, jnp.float32, jnp.int32
NX, NY, NZ = 4, 8, 8
WIDE = NX * NY * 2
EDGES, WIDTH, TRIP, BASIS, TRIPLETS, SLOTS = 256, 1024, 64, 16, 32, 32
ATOMS, ATOM_WIDTH, HALF, TILE = 512, 512, 256, 128
GROUP = 32


def silu(value):
    return value / (1.0 + jnp.exp(-value))


def dot(a, b):
    return jnp.dot(a, b, preferred_element_type=F32)


def iota(shape, dim):
    return lax.broadcasted_iota(I32, shape, dim)


def dot_t(a, b):
    return lax.dot_general(a, b, (((1,), (1,)), ((), ())), preferred_element_type=F32)


def ones_where(mask):
    return jnp.where(mask, 1.0, 0.0).astype(BF16)


def remote(src, dst, send_sem, recv_sem, device):
    return pltpu.make_async_remote_copy(
        src_ref=src, dst_ref=dst, send_sem=send_sem, recv_sem=recv_sem,
        device_id=device, device_id_type=MESH,
    )


def kernel(
    source_ref, target_ref, gain_ref, msg_hbm, rows_hbm, w_down_hbm, basis_hbm, slot_hbm, w_bil_hbm, w_up_hbm,
    w_in_hbm, w_src_hbm, w_tgt_hbm, w_atom_hbm, atom_hbm,
    edge_out, atom_out,
    msg_ref, rows_ref, w_down_ref, basis_ref, slot_ref, w_bil_ref, w_up_ref, w_in_ref, w_src_ref, w_tgt_ref,
    w_atom_ref, atom_ref, load_sem,
    out_buf, in_buf, table, spread, bands, digit_buf, group_buf, hot_buf, mixed, send_sem, recv_sem, mid_ref, part_ref,
    snd1, rcv1, snd2, rcv2, snd3, rcv3, snd4, rcv4, all_a, all_b, sib_a, sib_b, src_sib, pick_snd, pick_rcv, col,
    s1, r1, s2, r2, s3, r3, s4, r4, si, ri, sa1, ra1, sb1, rb1, sring, rring, sfar, rfar, sshare, rshare, so, ro, sp, rp,
):
    me, row = lax.axis_index("wide"), lax.axis_index("narrow")
    x, y, c, z = me // 16, (me // 2) % NY, me % 2, row
    other = 1 - c
    barrier = pltpu.get_barrier_semaphore()

    def at(px, py, pc, pz):
        return (px * 16 + py * 2 + pc, pz)

    sibling = at(x, y, other, z)
    xs = [(lax.rem(x + i, NX), i) for i in range(1, NX)]
    ys = [(lax.rem(y + i, NY), i) for i in range(1, NY)]
    zs = [(lax.rem(z + i, NZ), i) for i in range(1, NZ)]
    place_a, place_b = x * NY + y, x * NZ + z
    waiting = []

    def start(copy):
        copy.start()
        waiting.append(copy)

    def drain(keep):
        while len(waiting) > keep:
            waiting.pop(0).wait_send()

    mine, theirs = pl.ds(pl.multiple_of(c * HALF, HALF), HALF), pl.ds(pl.multiple_of(other * HALF, HALF), HALF)
    my_rows = pl.ds(pl.multiple_of(x * TILE + y * 16, 16), 16)
    pairs = [
        (msg_hbm, msg_ref), (w_down_hbm, w_down_ref), (rows_hbm, rows_ref), (basis_hbm, basis_ref),
        (slot_hbm, slot_ref), (w_bil_hbm, w_bil_ref), (w_up_hbm, w_up_ref), (w_in_hbm, w_in_ref),
        (w_atom_hbm.at[:, mine], w_atom_ref), (atom_hbm.at[my_rows, mine], atom_ref),
        (w_src_hbm, w_src_ref), (w_tgt_hbm, w_tgt_ref),
    ]
    loads = [pltpu.make_async_copy(a, b, load_sem.at[i]) for i, (a, b) in enumerate(pairs)]
    for load in loads:
        load.start()

    def greet(i, carry):
        pl.semaphore_signal(barrier, inc=1, device_id=(lax.rem(me + i, WIDE), row), device_id_type=MESH)
        return carry

    lax.fori_loop(1, WIDE, greet, 0)
    for px in range(NX):
        for p, _ in zs:
            pl.semaphore_signal(barrier, inc=1, device_id=at(px, y, c, p), device_id_type=MESH)
    for load in loads[:3]:
        load.wait()

    down = silu(dot_t(w_down_ref[...], msg_ref[...]))
    twice = jnp.concatenate([down, down], axis=0).astype(BF16)
    low_lane = iota((16, TILE), 1) < TRIP
    for j in range(8):
        hot = ones_where(iota((EDGES, 256), 0) == rows_ref[:, j * 256 : (j + 1) * 256])
        picked = dot(twice, hot).T
        for p in range(8):
            first, second = picked[p * 32 : p * 32 + 16], picked[p * 32 + 16 : p * 32 + 32]
            out_buf[j * 8 + p] = jnp.where(low_lane, first, second).astype(BF16)

    pl.semaphore_wait(barrier, WIDE - 1 + NX * (NZ - 1))
    start(remote(source_ref, src_sib, si, ri, sibling))
    def copy_to(i):
        peer = lax.rem(me + i, WIDE)
        return peer, remote(out_buf.at[peer], in_buf.at[me], send_sem.at[peer], recv_sem.at[me], (peer, row))

    def send(i, carry):
        copy_to(i)[1].start()
        return carry

    lax.fori_loop(1, WIDE, send, 0)
    in_buf[me] = out_buf[me]

    for load in loads[3:5]:
        load.wait()
    spread[...] = ones_where((iota((512, 256), 0) >> 4) == (iota((512, 256), 1) & 31))
    key = iota((8, 512), 1) & 15
    band = (iota((TILE, 256), 0) & 7) == (iota((TILE, 256), 1) >> 5)

    def build(i, carry):
        two = basis_ref[pl.ds(pl.multiple_of(i * 16, 16), 16), :].astype(F32)
        for h in range(2):
            x = two[h * 8 : h * 8 + 8]
            tall = jnp.concatenate([jnp.where(key == k, x, 0.0) for k in range(BASIS)], axis=0)
            block = jnp.where(band, dot(tall.astype(BF16), spread[...]), 0.0)
            bands[pl.ds(pl.multiple_of(i * 256 + h * TILE, TILE), TILE), :] = block.astype(BF16)
        return carry

    lax.fori_loop(0, EDGES // 16, build, 0, unroll=2)

    slots = slot_ref[...]
    parts = [(slots >> 5) & 31, slots & 15, ((slots >> 10) << 1) | ((slots >> 4) & 1), slots * 0]
    digits = jnp.concatenate(parts, axis=0).astype(F32).T
    digit = iota((TILE, 256), 0) >> 5
    left = iota((TILE, 256), 1) < TILE
    weigh = jnp.where(left & (digit == 0), 16.0, jnp.where(digit == jnp.where(left, 1, 2), 1.0, 0.0)).astype(BF16)
    own_digit = (iota((TRIPLETS, TILE), 1) & 31) == iota((TRIPLETS, TILE), 0)
    digit_buf[...] = digits
    lane = iota((256, TILE), 1).astype(F32)

    def place(i, carry):
        few = digit_buf[pl.ds(pl.multiple_of(i * 8, 8), 8), :]
        tall = [jnp.where(own_digit, few[e : e + 1], 0.0) for e in range(8)]
        found = dot(jnp.concatenate(tall, axis=0).astype(BF16), weigh)
        lines = pl.ds(pl.multiple_of(i * 256, 256), 256)
        hot = [ones_where(found[:, :TILE] == lane + float(j * TILE)) for j in range(4)]
        hot_buf[lines, :] = jnp.concatenate(hot, axis=1)
        group_buf[lines, :] = found[:, TILE:]
        return carry

    lax.fori_loop(0, EDGES // 8, place, 0, unroll=2)

    remote(source_ref, src_sib, si, ri, sibling).wait_recv()
    for i, ref in enumerate((source_ref, src_sib, target_ref)):
        for h in range(2):
            line = ref[:, h * TILE : (h + 1) * TILE].astype(F32)
            turned = jnp.broadcast_to(line, (TILE, TILE)).T
            col[i * 2 + h] = turned.astype(I32)

    def arrived(i, carry):
        peer = lax.rem(me + i, WIDE)
        remote(out_buf.at[peer], in_buf.at[peer], send_sem.at[peer], recv_sem.at[peer], (peer, row)).wait_recv()
        return carry

    lax.fori_loop(1, WIDE, arrived, 0)

    received = in_buf[...].reshape(WIDE * 16, TILE)
    table[...] = jnp.concatenate([received[:512], received[512:]], axis=1)
    low_lane8 = iota((8, TILE), 1) < TRIP
    lane_half = (iota((GROUP * TRIPLETS, TILE), 1) >> 6).astype(F32)

    def mix(i, carry):
        lines = pl.ds(pl.multiple_of(i * GROUP * TRIPLETS, GROUP * TRIPLETS), GROUP * TRIPLETS)
        four, g = dot(hot_buf[lines, :], table[...]), group_buf[lines, :]
        rows = jnp.where(g == lane_half, four[:, :TILE], 0.0) + jnp.where(g == lane_half + 2.0, four[:, TILE:], 0.0)
        rows = rows.astype(BF16)
        for b in range(GROUP // 8):
            block = bands[pl.ds(pl.multiple_of((i * (GROUP // 8) + b) * TILE, TILE), TILE), :]
            got = dot(block, rows[b * 256 : (b + 1) * 256])
            got = got + pltpu.roll(got, TRIP, 1)
            for k in range(8):
                pair = jnp.where(low_lane8, got[k * 16 : k * 16 + 8], got[k * 16 + 8 : k * 16 + 16])
                mixed[pl.ds(pl.multiple_of(i * GROUP + b * 8, 8), 8), k * TILE : (k + 1) * TILE] = pair
        return carry

    lax.fori_loop(0, EDGES // GROUP, mix, 0)

    for load in loads[5:]:
        load.wait()
    trip = silu(dot_t(mixed[...].astype(BF16), w_bil_ref[...])).astype(BF16)
    mid = (msg_ref[...].astype(F32) + dot(trip, w_up_ref[...])).astype(BF16)
    mid_ref[...] = mid
    message = dot(mid, w_in_ref[...]).astype(BF16)
    hot = ones_where(iota((ATOMS, EDGES), 0) == target_ref[...] - row * ATOMS)
    part_ref[...] = dot(hot, message)

    my_x = pl.ds(pl.multiple_of(x * TILE, TILE), TILE)
    order = [p for p, _ in xs] + [x]

    def chip_copy(i, p):
        return remote(snd1.at[i], rcv1.at[i], s1.at[i], r1.at[i], sibling)

    for i, p in enumerate(order):
        snd1[i] = part_ref[pl.ds(pl.multiple_of(p * TILE, TILE), TILE), theirs].astype(BF16)
        start(chip_copy(i, p))
    def sent(i, carry):
        copy_to(i)[1].wait_send()
        return carry

    lax.fori_loop(1, WIDE, sent, 0)
    for i, p in enumerate(order):
        chip_copy(i, p).wait_recv()
        if i < NX - 1:
            rows = part_ref[pl.ds(pl.multiple_of(p * TILE, TILE), TILE), mine] + rcv1[i].astype(F32)
            snd2[i] = rows.astype(BF16)
            start(remote(snd2.at[i], rcv2.at[x], s2.at[i], r2.at[x], at(p, y, c, z)))
    total = part_ref[my_x, mine] + rcv1[NX - 1].astype(F32)
    for p, _ in xs:
        remote(snd2.at[0], rcv2.at[p], s2.at[0], r2.at[p], at(p, y, c, z)).wait_recv()
        total = total + rcv2[p].astype(F32)
    snd3[...] = total.astype(BF16).reshape(NY, 16, HALF)
    for p, _ in ys:
        start(remote(snd3.at[p], rcv3.at[y], s3.at[p], r3.at[y], at(x, p, c, z)))
    share = snd3[y].astype(F32)
    for p, _ in ys:
        remote(snd3.at[p], rcv3.at[p], s3.at[p], r3.at[p], at(x, p, c, z)).wait_recv()
        share = share + rcv3[p].astype(F32)
    snd4[...] = share
    start(remote(snd4, rcv4, s4, r4, sibling))


    remote(snd4, rcv4, s4, r4, sibling).wait_recv()
    theirs4 = rcv4[...]
    squares = jnp.sum(share * share, axis=-1, keepdims=True) + jnp.sum(theirs4 * theirs4, axis=-1, keepdims=True)
    scale = lax.rsqrt(squares * (1.0 / ATOM_WIDTH) + 1e-06)
    norm_mine = (share * scale * gain_ref[:, mine]).astype(BF16)
    norm_theirs = (theirs4 * scale * gain_ref[:, theirs]).astype(BF16)
    grown = silu(dot(norm_mine, w_atom_ref[mine, :]) + dot(norm_theirs, w_atom_ref[theirs, :]))
    fresh = (atom_ref[...].astype(F32) + grown).astype(BF16)
    all_a[z, x, y] = fresh[:, :TILE]
    all_b[z, x, y] = fresh[:, TILE:]

    def plane_copies(i, sending):
        a, b = lax.rem(place_a + i, NX * NY), lax.rem(place_b + i, NX * NZ)
        ax, ay, bx, bz = a // NY, a % NY, b // NZ, b % NZ
        view_a = all_a.at[z, x, y] if sending else all_a.at[z, ax, ay]
        view_b = all_b.at[z, x, y] if sending else all_b.at[bz, bx, y]
        return (
            remote(view_a, view_a, sa1.at[a], ra1.at[place_a if sending else a], at(ax, ay, c, z)),
            remote(view_b, view_b, sb1.at[b], rb1.at[place_b if sending else b], at(bx, y, c, bz)),
        )

    def plane_send(i, carry):
        for copy in plane_copies(i, True):
            copy.start()
        return carry

    def plane_arrived(i, carry):
        for copy in plane_copies(i, False):
            copy.wait_recv()
        return carry

    def plane_sent(i, carry):
        for copy in plane_copies(i, True):
            copy.wait_send()
        return carry

    lax.fori_loop(1, NX * NY, plane_send, 0)
    lax.fori_loop(1, NX * NY, plane_arrived, 0)

    def ring_copy(axis, way, step, part, sending):
        n, pos = (NZ, z) if axis == 0 else (NY, y)
        hop = 1 if way == 0 else n - 1
        back = step - 1 if sending else step
        block = lax.rem(pos + (n - back if way == 0 else back), n)
        view = all_a.at[block, part] if axis == 0 else all_b.at[:, part, block]
        to = lax.rem(pos + hop, n)
        device = at(x, y, c, to) if axis == 0 else at(x, to, c, z)
        index = ((axis * 2 + way) * 4 + step - 1) * NX + part
        return remote(view, view, sring.at[index], rring.at[index], device)

    across = lax.rem(z + 4, NZ), lax.rem(y + 4, NY)

    def quarter(axis, block, part):
        return all_a.at[block, part] if axis == 0 else all_b.at[:, part, block]

    def far_copy(axis, sending):
        view = quarter(axis, (z if axis == 0 else y) if sending else across[axis], x)
        device = at(x, y, c, across[0]) if axis == 0 else at(x, across[1], c, z)
        return remote(view, view, sfar.at[axis], rfar.at[axis], device)

    def share_copy(axis, p, sending):
        view = quarter(axis, across[axis], x if sending else p)
        return remote(view, view, sshare.at[axis * NX + p], rshare.at[axis * NX + (x if sending else p)], at(p, y, c, z))

    for axis in (1, 0):
        start(far_copy(axis, True))
    for part in range(NX):
        for axis in (1, 0):
            for way in range(2):
                start(ring_copy(axis, way, 1, part, True))
    own_a = remote(all_a.at[z], sib_a, so.at[0], ro.at[0], sibling)
    start(own_a)
    lax.fori_loop(1, NX * NY, plane_sent, 0)
    drain(19)
    for step in range(1, 4):
        for part in range(NX):
            for axis in (1, 0):
                for way in range(2):
                    ring_copy(axis, way, step, part, False).wait_recv()
                    if step < 3:
                        start(ring_copy(axis, way, step + 1, part, True))
        if step == 1:
            for axis in (1, 0):
                far_copy(axis, False).wait_recv()
                for p, _ in xs:
                    start(share_copy(axis, p, True))
        if step < 3:
            drain(22)
    for axis in (1, 0):
        for p, _ in xs:
            share_copy(axis, p, False).wait_recv()
    own_b = remote(all_b.at[z], sib_b, so.at[1], ro.at[1], sibling)
    start(own_b)

    lanes = iota((EDGES, ATOMS), 1)

    def column(i):
        halves = [jnp.concatenate([col[i * 2 + h]] * (ATOMS // TILE), axis=1) for h in range(2)]
        return jnp.concatenate(halves, axis=0)

    def rows_of(first_ref, second_ref):
        a, b = first_ref[...].reshape(ATOMS, TILE), second_ref[...].reshape(ATOMS, TILE)
        return jnp.concatenate([a, b], axis=1)

    def picked(i):
        total = jnp.zeros((EDGES, HALF), F32)
        for block in range(NZ):
            hot = ones_where(column(i) - block * ATOMS == lanes)
            total = total + dot(hot, rows_of(all_a.at[block], all_b.at[block]))
        return total.astype(BF16)

    pick_snd[...] = picked(1)
    start(remote(pick_snd, pick_rcv, sp, rp, sibling))
    update = dot(picked(0), w_src_ref[mine, :])
    own_a.wait_recv()
    own_b.wait_recv()
    hot = ones_where(column(2) - z * ATOMS == lanes)
    ours = rows_of(all_a.at[z], all_b.at[z])
    sibs = rows_of(sib_a, sib_b)
    atom_out[:, mine] = ours
    atom_out[:, theirs] = sibs
    update += dot(dot(hot, ours).astype(BF16), w_tgt_ref[mine, :])
    update += dot(dot(hot, sibs).astype(BF16), w_tgt_ref[theirs, :])
    drain(1)
    remote(pick_snd, pick_rcv, sp, rp, sibling).wait_recv()
    update += dot(pick_rcv[...], w_src_ref[theirs, :])
    edge_out[...] = (mid_ref[...].astype(F32) + silu(update)).astype(BF16)
    drain(0)


def dma(*shape):
    return pltpu.SemaphoreType.DMA(shape)


def per_device(
    edge_msg, basis, atom_h, edge_source, edge_target, send_rows, trip_slot,
    w_down, w_bil, w_up, w_atom_in, atom_gain, w_atom, w_src, w_tgt,
):
    vmem = pl.BlockSpec(memory_space=pltpu.VMEM)
    hbm = pl.BlockSpec(memory_space=pltpu.HBM)

    def every():
        return pltpu.VMEM((NZ, NX, NY, 16, TILE), BF16)

    def one():
        return pltpu.VMEM((NX, NY, 16, TILE), BF16)

    def semaphores(n):
        return [pltpu.SemaphoreType.DMA] * n

    edge_out, atom_out = pl.pallas_call(
        kernel,
        out_shape=(
            jax.ShapeDtypeStruct((EDGES, WIDTH), BF16),
            jax.ShapeDtypeStruct((ATOMS, ATOM_WIDTH), BF16),
        ),
        in_specs=[vmem] * 3 + [hbm] * 12,
        out_specs=(vmem, vmem),
        scratch_shapes=[
            pltpu.VMEM((EDGES, WIDTH), BF16),
            pltpu.VMEM((1, WIDE * SLOTS), I32),
            pltpu.VMEM((TRIP, WIDTH), BF16),
            pltpu.VMEM((EDGES, TRIPLETS * BASIS), BF16),
            pltpu.VMEM((TRIPLETS, EDGES), I32),
            pltpu.VMEM((TRIP, BASIS * TRIP), BF16),
            pltpu.VMEM((TRIP, WIDTH), BF16),
            pltpu.VMEM((WIDTH, ATOM_WIDTH), BF16),
            pltpu.VMEM((ATOM_WIDTH, WIDTH), BF16),
            pltpu.VMEM((ATOM_WIDTH, WIDTH), BF16),
            pltpu.VMEM((ATOM_WIDTH, HALF), BF16),
            pltpu.VMEM((16, HALF), BF16),
            dma(12),
            pltpu.VMEM((WIDE, 16, TILE), BF16),
            pltpu.VMEM((WIDE, 16, TILE), BF16),
            pltpu.VMEM((512, 256), BF16),
            pltpu.VMEM((512, 256), BF16),
            pltpu.VMEM((EDGES * BASIS, 256), BF16),
            pltpu.VMEM((EDGES, TILE), F32),
            pltpu.VMEM((EDGES * TRIPLETS, TILE), F32),
            pltpu.VMEM((EDGES * TRIPLETS, 512), BF16),
            pltpu.VMEM((EDGES, BASIS * TRIP), F32),
            dma(WIDE),
            dma(WIDE),
            pltpu.VMEM((EDGES, WIDTH), BF16),
            pltpu.VMEM((ATOMS, ATOM_WIDTH), F32),
            pltpu.VMEM((NX, TILE, HALF), BF16), pltpu.VMEM((NX, TILE, HALF), BF16),
            pltpu.VMEM((NX, NY * 16, HALF), BF16), pltpu.VMEM((NX, NY * 16, HALF), BF16),
            pltpu.VMEM((NY, 16, HALF), BF16), pltpu.VMEM((NY, 16, HALF), BF16),
            pltpu.VMEM((16, HALF), F32), pltpu.VMEM((16, HALF), F32),
            every(), every(), one(), one(),
            pltpu.VMEM((1, EDGES), I32),
            pltpu.VMEM((EDGES, HALF), BF16), pltpu.VMEM((EDGES, HALF), BF16),
            pltpu.VMEM((6, TILE, TILE), I32),
            dma(NX), dma(NX), dma(NX), dma(NX), dma(NY), dma(NY),
            *semaphores(4),
            dma(NX * NY), dma(NX * NY), dma(NX * NZ), dma(NX * NZ),
            dma(64), dma(64), dma(2), dma(2), dma(2 * NX), dma(2 * NX), dma(2), dma(2),
            *semaphores(2),
        ],
        compiler_params=pltpu.CompilerParams(
            collective_id=0, has_side_effects=True, vmem_limit_bytes=60 * 1024 * 1024
        ),
        name="block",
    )(
        edge_source.reshape(1, EDGES), edge_target.reshape(1, EDGES), atom_gain.reshape(1, ATOM_WIDTH),
        edge_msg, send_rows, w_down.T, basis, trip_slot.T, w_bil.T, w_up, w_atom_in, w_src, w_tgt, w_atom, atom_h,
    )
    return edge_out, atom_out


def solution(mesh):
    placed = (
        P(("wide", "narrow"), None),
        P(("wide", "narrow"), None),
        P("narrow", None),
        P(("wide", "narrow")),
        P(("wide", "narrow")),
        P(("wide", "narrow"), None),
        P(("wide", "narrow"), None),
        P(), P(), P(), P(), P(), P(), P(), P(),
    )
    return jax.shard_map(
        per_device,
        mesh=mesh,
        in_specs=placed,
        out_specs=(P(("wide", "narrow"), None), P("narrow", None)),
        check_vma=False,
    )
```

```python
import jax
import jax.numpy as jnp
from jax import lax
from jax.experimental import pallas as pl
from jax.experimental.pallas import tpu as pltpu
from jax.sharding import PartitionSpec as P

MESH = pl.DeviceIdType.MESH
BF16, F32, I32 = jnp.bfloat16, jnp.float32, jnp.int32
NX, NY, NZ = 4, 8, 8
WIDE = NX * NY * 2
EDGES, WIDTH, TRIP, BASIS, TRIPLETS, SLOTS = 256, 1024, 64, 16, 32, 32
ATOMS, ATOM_WIDTH, HALF, TILE = 512, 512, 256, 128
GROUP = 32


def silu(value):
    return value / (1.0 + jnp.exp(-value))


def dot(a, b):
    return jnp.dot(a, b, preferred_element_type=F32)


def iota(shape, dim):
    return lax.broadcasted_iota(I32, shape, dim)


def dot_t(a, b):
    return lax.dot_general(a, b, (((1,), (1,)), ((), ())), preferred_element_type=F32)


def ones_where(mask):
    return jnp.where(mask, 1.0, 0.0).astype(BF16)


def remote(src, dst, send_sem, recv_sem, device):
    return pltpu.make_async_remote_copy(
        src_ref=src, dst_ref=dst, send_sem=send_sem, recv_sem=recv_sem,
        device_id=device, device_id_type=MESH,
    )


def kernel(
    source_ref, target_ref, gain_ref, msg_hbm, rows_hbm, w_down_hbm, basis_hbm, slot_hbm, w_bil_hbm, w_up_hbm,
    w_in_hbm, w_src_hbm, w_tgt_hbm, w_atom_hbm, atom_hbm,
    edge_out, atom_out,
    msg_ref, rows_ref, w_down_ref, basis_ref, slot_ref, w_bil_ref, w_up_ref, w_in_ref, w_src_ref, w_tgt_ref,
    w_atom_ref, atom_ref, load_sem,
    out_buf, in_buf, table, spread, bands, digit_buf, group_buf, hot_buf, mixed, send_sem, recv_sem, mid_ref, part_ref,
    snd1, rcv1, snd2, rcv2, snd3, rcv3, snd4, rcv4, all_a, all_b, sib_a, sib_b, src_sib, pick_snd, pick_rcv, col,
    s1, r1, s2, r2, s3, r3, s4, r4, si, ri, sa1, ra1, sb1, rb1, sring, rring, sfar, rfar, sshare, rshare, so, ro, sp, rp,
):
    me, row = lax.axis_index("wide"), lax.axis_index("narrow")
    x, y, c, z = me // 16, (me // 2) % NY, me % 2, row
    other = 1 - c
    barrier = pltpu.get_barrier_semaphore()

    def at(px, py, pc, pz):
        return (px * 16 + py * 2 + pc, pz)

    sibling = at(x, y, other, z)
    xs = [(lax.rem(x + i, NX), i) for i in range(1, NX)]
    ys = [(lax.rem(y + i, NY), i) for i in range(1, NY)]
    zs = [(lax.rem(z + i, NZ), i) for i in range(1, NZ)]
    place_a, place_b = x * NY + y, x * NZ + z
    waiting = []

    def start(copy):
        copy.start()
        waiting.append(copy)

    def drain(keep):
        while len(waiting) > keep:
            waiting.pop(0).wait_send()

    mine, theirs = pl.ds(pl.multiple_of(c * HALF, HALF), HALF), pl.ds(pl.multiple_of(other * HALF, HALF), HALF)
    my_rows = pl.ds(pl.multiple_of(x * TILE + y * 16, 16), 16)
    pairs = [
        (msg_hbm, msg_ref), (w_down_hbm, w_down_ref), (rows_hbm, rows_ref), (basis_hbm, basis_ref),
        (slot_hbm, slot_ref), (w_bil_hbm, w_bil_ref), (w_up_hbm, w_up_ref), (w_in_hbm, w_in_ref),
        (w_atom_hbm.at[:, mine], w_atom_ref), (atom_hbm.at[my_rows, mine], atom_ref),
        (w_src_hbm, w_src_ref), (w_tgt_hbm, w_tgt_ref),
    ]
    loads = [pltpu.make_async_copy(a, b, load_sem.at[i]) for i, (a, b) in enumerate(pairs)]
    for load in loads:
        load.start()

    def greet(i, carry):
        pl.semaphore_signal(barrier, inc=1, device_id=(lax.rem(me + i, WIDE), row), device_id_type=MESH)
        return carry

    lax.fori_loop(1, WIDE, greet, 0, unroll=7)
    for px in range(NX):
        for p, _ in zs:
            pl.semaphore_signal(barrier, inc=1, device_id=at(px, y, c, p), device_id_type=MESH)
    for load in loads[:3]:
        load.wait()

    down = silu(dot_t(w_down_ref[...], msg_ref[...]))
    twice = jnp.concatenate([down, down], axis=0).astype(BF16)
    low_lane = iota((16, TILE), 1) < TRIP
    for j in range(8):
        hot = ones_where(iota((EDGES, 256), 0) == rows_ref[:, j * 256 : (j + 1) * 256])
        picked = dot(twice, hot).T
        for p in range(8):
            first, second = picked[p * 32 : p * 32 + 16], picked[p * 32 + 16 : p * 32 + 32]
            out_buf[j * 8 + p] = jnp.where(low_lane, first, second).astype(BF16)

    pl.semaphore_wait(barrier, WIDE - 1 + NX * (NZ - 1))
    start(remote(source_ref, src_sib, si, ri, sibling))
    def copy_to(i):
        peer = lax.rem(me + i, WIDE)
        return peer, remote(out_buf.at[peer], in_buf.at[me], send_sem.at[peer], recv_sem.at[me], (peer, row))

    def send(i, carry):
        copy_to(i)[1].start()
        return carry

    lax.fori_loop(1, WIDE, send, 0, unroll=7)
    in_buf[me] = out_buf[me]

    for load in loads[3:5]:
        load.wait()
    spread[...] = ones_where((iota((512, 256), 0) >> 4) == (iota((512, 256), 1) & 31))
    key = iota((8, 512), 1) & 15
    band = (iota((TILE, 256), 0) & 7) == (iota((TILE, 256), 1) >> 5)

    def build(i, carry):
        two = basis_ref[pl.ds(pl.multiple_of(i * 16, 16), 16), :].astype(F32)
        for h in range(2):
            x = two[h * 8 : h * 8 + 8]
            tall = jnp.concatenate([jnp.where(key == k, x, 0.0) for k in range(BASIS)], axis=0)
            block = jnp.where(band, dot(tall.astype(BF16), spread[...]), 0.0)
            bands[pl.ds(pl.multiple_of(i * 256 + h * TILE, TILE), TILE), :] = block.astype(BF16)
        return carry

    lax.fori_loop(0, EDGES // 16, build, 0, unroll=2)

    slots = slot_ref[...]
    parts = [(slots >> 5) & 31, slots & 15, ((slots >> 10) << 1) | ((slots >> 4) & 1), slots * 0]
    digits = jnp.concatenate(parts, axis=0).astype(F32).T
    digit = iota((TILE, 256), 0) >> 5
    left = iota((TILE, 256), 1) < TILE
    weigh = jnp.where(left & (digit == 0), 16.0, jnp.where(digit == jnp.where(left, 1, 2), 1.0, 0.0)).astype(BF16)
    own_digit = (iota((TRIPLETS, TILE), 1) & 31) == iota((TRIPLETS, TILE), 0)
    digit_buf[...] = digits
    lane = iota((256, TILE), 1).astype(F32)

    def place(i, carry):
        few = digit_buf[pl.ds(pl.multiple_of(i * 8, 8), 8), :]
        tall = [jnp.where(own_digit, few[e : e + 1], 0.0) for e in range(8)]
        found = dot(jnp.concatenate(tall, axis=0).astype(BF16), weigh)
        lines = pl.ds(pl.multiple_of(i * 256, 256), 256)
        hot = [ones_where(found[:, :TILE] == lane + float(j * TILE)) for j in range(4)]
        hot_buf[lines, :] = jnp.concatenate(hot, axis=1)
        group_buf[lines, :] = found[:, TILE:]
        return carry

    lax.fori_loop(0, EDGES // 8, place, 0, unroll=2)

    remote(source_ref, src_sib, si, ri, sibling).wait_recv()
    for i, ref in enumerate((source_ref, src_sib, target_ref)):
        for h in range(2):
            line = ref[:, h * TILE : (h + 1) * TILE].astype(F32)
            turned = jnp.broadcast_to(line, (TILE, TILE)).T
            col[i * 2 + h] = turned.astype(I32)

    def arrived(i, carry):
        peer = lax.rem(me + i, WIDE)
        remote(out_buf.at[peer], in_buf.at[peer], send_sem.at[peer], recv_sem.at[peer], (peer, row)).wait_recv()
        return carry

    lax.fori_loop(1, WIDE, arrived, 0, unroll=7)

    received = in_buf[...].reshape(WIDE * 16, TILE)
    table[...] = jnp.concatenate([received[:512], received[512:]], axis=1)
    low_lane8 = iota((8, TILE), 1) < TRIP
    lane_half = (iota((GROUP * TRIPLETS, TILE), 1) >> 6).astype(F32)

    def mix(i, carry):
        lines = pl.ds(pl.multiple_of(i * GROUP * TRIPLETS, GROUP * TRIPLETS), GROUP * TRIPLETS)
        four, g = dot(hot_buf[lines, :], table[...]), group_buf[lines, :]
        rows = jnp.where(g == lane_half, four[:, :TILE], 0.0) + jnp.where(g == lane_half + 2.0, four[:, TILE:], 0.0)
        rows = rows.astype(BF16)
        for b in range(GROUP // 8):
            block = bands[pl.ds(pl.multiple_of((i * (GROUP // 8) + b) * TILE, TILE), TILE), :]
            got = dot(block, rows[b * 256 : (b + 1) * 256])
            got = got + pltpu.roll(got, TRIP, 1)
            for k in range(8):
                pair = jnp.where(low_lane8, got[k * 16 : k * 16 + 8], got[k * 16 + 8 : k * 16 + 16])
                mixed[pl.ds(pl.multiple_of(i * GROUP + b * 8, 8), 8), k * TILE : (k + 1) * TILE] = pair
        return carry

    lax.fori_loop(0, EDGES // GROUP, mix, 0)

    for load in loads[5:]:
        load.wait()
    trip = silu(dot_t(mixed[...].astype(BF16), w_bil_ref[...])).astype(BF16)
    mid = (msg_ref[...].astype(F32) + dot(trip, w_up_ref[...])).astype(BF16)
    mid_ref[...] = mid
    message = dot(mid, w_in_ref[...]).astype(BF16)
    hot = ones_where(iota((ATOMS, EDGES), 0) == target_ref[...] - row * ATOMS)
    part_ref[...] = dot(hot, message)

    my_x = pl.ds(pl.multiple_of(x * TILE, TILE), TILE)
    order = [p for p, _ in xs] + [x]

    def chip_copy(i, p):
        return remote(snd1.at[i], rcv1.at[i], s1.at[i], r1.at[i], sibling)

    for i, p in enumerate(order):
        snd1[i] = part_ref[pl.ds(pl.multiple_of(p * TILE, TILE), TILE), theirs].astype(BF16)
        start(chip_copy(i, p))
    def sent(i, carry):
        copy_to(i)[1].wait_send()
        return carry

    lax.fori_loop(1, WIDE, sent, 0)
    for i, p in enumerate(order):
        chip_copy(i, p).wait_recv()
        if i < NX - 1:
            rows = part_ref[pl.ds(pl.multiple_of(p * TILE, TILE), TILE), mine] + rcv1[i].astype(F32)
            snd2[i] = rows.astype(BF16)
            start(remote(snd2.at[i], rcv2.at[x], s2.at[i], r2.at[x], at(p, y, c, z)))
    total = part_ref[my_x, mine] + rcv1[NX - 1].astype(F32)
    for p, _ in xs:
        remote(snd2.at[0], rcv2.at[p], s2.at[0], r2.at[p], at(p, y, c, z)).wait_recv()
        total = total + rcv2[p].astype(F32)
    snd3[...] = total.astype(BF16).reshape(NY, 16, HALF)
    for p, _ in ys:
        start(remote(snd3.at[p], rcv3.at[y], s3.at[p], r3.at[y], at(x, p, c, z)))
    share = snd3[y].astype(F32)
    for p, _ in ys:
        remote(snd3.at[p], rcv3.at[p], s3.at[p], r3.at[p], at(x, p, c, z)).wait_recv()
        share = share + rcv3[p].astype(F32)
    snd4[...] = share
    start(remote(snd4, rcv4, s4, r4, sibling))


    remote(snd4, rcv4, s4, r4, sibling).wait_recv()
    theirs4 = rcv4[...]
    squares = jnp.sum(share * share, axis=-1, keepdims=True) + jnp.sum(theirs4 * theirs4, axis=-1, keepdims=True)
    scale = lax.rsqrt(squares * (1.0 / ATOM_WIDTH) + 1e-06)
    norm_mine = (share * scale * gain_ref[:, mine]).astype(BF16)
    norm_theirs = (theirs4 * scale * gain_ref[:, theirs]).astype(BF16)
    grown = silu(dot(norm_mine, w_atom_ref[mine, :]) + dot(norm_theirs, w_atom_ref[theirs, :]))
    fresh = (atom_ref[...].astype(F32) + grown).astype(BF16)
    all_a[z, x, y] = fresh[:, :TILE]
    all_b[z, x, y] = fresh[:, TILE:]

    def plane_copies(i, sending):
        a, b = lax.rem(place_a + i, NX * NY), lax.rem(place_b + i, NX * NZ)
        ax, ay, bx, bz = a // NY, a % NY, b // NZ, b % NZ
        view_a = all_a.at[z, x, y] if sending else all_a.at[z, ax, ay]
        view_b = all_b.at[z, x, y] if sending else all_b.at[bz, bx, y]
        return (
            remote(view_a, view_a, sa1.at[a], ra1.at[place_a if sending else a], at(ax, ay, c, z)),
            remote(view_b, view_b, sb1.at[b], rb1.at[place_b if sending else b], at(bx, y, c, bz)),
        )

    def plane_send(i, carry):
        for copy in plane_copies(i, True):
            copy.start()
        return carry

    def plane_arrived(i, carry):
        for copy in plane_copies(i, False):
            copy.wait_recv()
        return carry

    def plane_sent(i, carry):
        for copy in plane_copies(i, True):
            copy.wait_send()
        return carry

    lax.fori_loop(1, NX * NY, plane_send, 0)
    lax.fori_loop(1, NX * NY, plane_arrived, 0)

    def ring_copy(axis, way, step, part, sending):
        n, pos = (NZ, z) if axis == 0 else (NY, y)
        hop = 1 if way == 0 else n - 1
        back = step - 1 if sending else step
        block = lax.rem(pos + (n - back if way == 0 else back), n)
        view = all_a.at[block, part] if axis == 0 else all_b.at[:, part, block]
        to = lax.rem(pos + hop, n)
        device = at(x, y, c, to) if axis == 0 else at(x, to, c, z)
        index = ((axis * 2 + way) * 4 + step - 1) * NX + part
        return remote(view, view, sring.at[index], rring.at[index], device)

    across = lax.rem(z + 4, NZ), lax.rem(y + 4, NY)

    def quarter(axis, block, part):
        return all_a.at[block, part] if axis == 0 else all_b.at[:, part, block]

    def far_copy(axis, sending):
        view = quarter(axis, (z if axis == 0 else y) if sending else across[axis], x)
        device = at(x, y, c, across[0]) if axis == 0 else at(x, across[1], c, z)
        return remote(view, view, sfar.at[axis], rfar.at[axis], device)

    def share_copy(axis, p, sending):
        view = quarter(axis, across[axis], x if sending else p)
        return remote(view, view, sshare.at[axis * NX + p], rshare.at[axis * NX + (x if sending else p)], at(p, y, c, z))

    for axis in (1, 0):
        start(far_copy(axis, True))
    for part in range(NX):
        for axis in (1, 0):
            for way in range(2):
                start(ring_copy(axis, way, 1, part, True))
    own_a = remote(all_a.at[z], sib_a, so.at[0], ro.at[0], sibling)
    start(own_a)
    lax.fori_loop(1, NX * NY, plane_sent, 0)
    drain(19)
    for step in range(1, 4):
        for part in range(NX):
            for axis in (1, 0):
                for way in range(2):
                    ring_copy(axis, way, step, part, False).wait_recv()
                    if step < 3:
                        start(ring_copy(axis, way, step + 1, part, True))
        if step == 1:
            for axis in (1, 0):
                far_copy(axis, False).wait_recv()
                for p, _ in xs:
                    start(share_copy(axis, p, True))
        if step < 3:
            drain(22)
    for axis in (1, 0):
        for p, _ in xs:
            share_copy(axis, p, False).wait_recv()
    own_b = remote(all_b.at[z], sib_b, so.at[1], ro.at[1], sibling)
    start(own_b)

    lanes = iota((EDGES, ATOMS), 1)

    def column(i):
        halves = [jnp.concatenate([col[i * 2 + h]] * (ATOMS // TILE), axis=1) for h in range(2)]
        return jnp.concatenate(halves, axis=0)

    def rows_of(first_ref, second_ref):
        a, b = first_ref[...].reshape(ATOMS, TILE), second_ref[...].reshape(ATOMS, TILE)
        return jnp.concatenate([a, b], axis=1)

    def picked(i):
        total = jnp.zeros((EDGES, HALF), F32)
        for block in range(NZ):
            hot = ones_where(column(i) - block * ATOMS == lanes)
            total = total + dot(hot, rows_of(all_a.at[block], all_b.at[block]))
        return total.astype(BF16)

    pick_snd[...] = picked(1)
    start(remote(pick_snd, pick_rcv, sp, rp, sibling))
    update = dot(picked(0), w_src_ref[mine, :])
    own_a.wait_recv()
    own_b.wait_recv()
    hot = ones_where(column(2) - z * ATOMS == lanes)
    ours = rows_of(all_a.at[z], all_b.at[z])
    sibs = rows_of(sib_a, sib_b)
    atom_out[:, mine] = ours
    atom_out[:, theirs] = sibs
    update += dot(dot(hot, ours).astype(BF16), w_tgt_ref[mine, :])
    update += dot(dot(hot, sibs).astype(BF16), w_tgt_ref[theirs, :])
    drain(1)
    remote(pick_snd, pick_rcv, sp, rp, sibling).wait_recv()
    update += dot(pick_rcv[...], w_src_ref[theirs, :])
    edge_out[...] = (mid_ref[...].astype(F32) + silu(update)).astype(BF16)
    drain(0)


def dma(*shape):
    return pltpu.SemaphoreType.DMA(shape)


def per_device(
    edge_msg, basis, atom_h, edge_source, edge_target, send_rows, trip_slot,
    w_down, w_bil, w_up, w_atom_in, atom_gain, w_atom, w_src, w_tgt,
):
    vmem = pl.BlockSpec(memory_space=pltpu.VMEM)
    hbm = pl.BlockSpec(memory_space=pltpu.HBM)

    def every():
        return pltpu.VMEM((NZ, NX, NY, 16, TILE), BF16)

    def one():
        return pltpu.VMEM((NX, NY, 16, TILE), BF16)

    def semaphores(n):
        return [pltpu.SemaphoreType.DMA] * n

    edge_out, atom_out = pl.pallas_call(
        kernel,
        out_shape=(
            jax.ShapeDtypeStruct((EDGES, WIDTH), BF16),
            jax.ShapeDtypeStruct((ATOMS, ATOM_WIDTH), BF16),
        ),
        in_specs=[vmem] * 3 + [hbm] * 12,
        out_specs=(vmem, vmem),
        scratch_shapes=[
            pltpu.VMEM((EDGES, WIDTH), BF16),
            pltpu.VMEM((1, WIDE * SLOTS), I32),
            pltpu.VMEM((TRIP, WIDTH), BF16),
            pltpu.VMEM((EDGES, TRIPLETS * BASIS), BF16),
            pltpu.VMEM((TRIPLETS, EDGES), I32),
            pltpu.VMEM((TRIP, BASIS * TRIP), BF16),
            pltpu.VMEM((TRIP, WIDTH), BF16),
            pltpu.VMEM((WIDTH, ATOM_WIDTH), BF16),
            pltpu.VMEM((ATOM_WIDTH, WIDTH), BF16),
            pltpu.VMEM((ATOM_WIDTH, WIDTH), BF16),
            pltpu.VMEM((ATOM_WIDTH, HALF), BF16),
            pltpu.VMEM((16, HALF), BF16),
            dma(12),
            pltpu.VMEM((WIDE, 16, TILE), BF16),
            pltpu.VMEM((WIDE, 16, TILE), BF16),
            pltpu.VMEM((512, 256), BF16),
            pltpu.VMEM((512, 256), BF16),
            pltpu.VMEM((EDGES * BASIS, 256), BF16),
            pltpu.VMEM((EDGES, TILE), F32),
            pltpu.VMEM((EDGES * TRIPLETS, TILE), F32),
            pltpu.VMEM((EDGES * TRIPLETS, 512), BF16),
            pltpu.VMEM((EDGES, BASIS * TRIP), F32),
            dma(WIDE),
            dma(WIDE),
            pltpu.VMEM((EDGES, WIDTH), BF16),
            pltpu.VMEM((ATOMS, ATOM_WIDTH), F32),
            pltpu.VMEM((NX, TILE, HALF), BF16), pltpu.VMEM((NX, TILE, HALF), BF16),
            pltpu.VMEM((NX, NY * 16, HALF), BF16), pltpu.VMEM((NX, NY * 16, HALF), BF16),
            pltpu.VMEM((NY, 16, HALF), BF16), pltpu.VMEM((NY, 16, HALF), BF16),
            pltpu.VMEM((16, HALF), F32), pltpu.VMEM((16, HALF), F32),
            every(), every(), one(), one(),
            pltpu.VMEM((1, EDGES), I32),
            pltpu.VMEM((EDGES, HALF), BF16), pltpu.VMEM((EDGES, HALF), BF16),
            pltpu.VMEM((6, TILE, TILE), I32),
            dma(NX), dma(NX), dma(NX), dma(NX), dma(NY), dma(NY),
            *semaphores(4),
            dma(NX * NY), dma(NX * NY), dma(NX * NZ), dma(NX * NZ),
            dma(64), dma(64), dma(2), dma(2), dma(2 * NX), dma(2 * NX), dma(2), dma(2),
            *semaphores(2),
        ],
        compiler_params=pltpu.CompilerParams(
            collective_id=0, has_side_effects=True, vmem_limit_bytes=60 * 1024 * 1024
        ),
        name="block",
    )(
        edge_source.reshape(1, EDGES), edge_target.reshape(1, EDGES), atom_gain.reshape(1, ATOM_WIDTH),
        edge_msg, send_rows, w_down.T, basis, trip_slot.T, w_bil.T, w_up, w_atom_in, w_src, w_tgt, w_atom, atom_h,
    )
    return edge_out, atom_out


def solution(mesh):
    placed = (
        P(("wide", "narrow"), None),
        P(("wide", "narrow"), None),
        P("narrow", None),
        P(("wide", "narrow")),
        P(("wide", "narrow")),
        P(("wide", "narrow"), None),
        P(("wide", "narrow"), None),
        P(), P(), P(), P(), P(), P(), P(), P(),
    )
    return jax.shard_map(
        per_device,
        mesh=mesh,
        in_specs=placed,
        out_specs=(P(("wide", "narrow"), None), P("narrow", None)),
        check_vma=False,
    )
```
